32 devices in a mesh: groups: 2 (over x), seq: 16 (over z, y, core).
Axes of the slice: x: 2, y: 2, z: 4, core: 2. Of those that a mesh axis runs over, the one named last changes fastest.
Arguments:
- self_query: bfloat16 [4096, 5120], P(('groups', 'seq')), parts along dimension 0, may hold values from -384 to 384
- self_key: bfloat16 [4096, 5120], P(('groups', 'seq')), parts along dimension 0, may hold values from -20 to 20
- self_value: bfloat16 [4096, 5120], P(('groups', 'seq')), parts along dimension 0, may hold values from -6 to 6
- cross_query: bfloat16 [4096, 5120], P(('groups', 'seq')), parts along dimension 0, may hold values from -384 to 384
- context: bfloat16 [512, 4096], P('groups'), parts along dimension 0, may hold values from -6 to 6
- key_weight: bfloat16 [4096, 5120], P(None, 'seq'), may hold values from -0.09375 to 0.09375
- value_weight: bfloat16 [4096, 5120], P(None, 'seq'), may hold values from -0.09375 to 0.09375
- band_width: int32 [40], replicated, may hold values from 0 to 15
Outputs:
- self_out: bfloat16 [4096, 5120], P(('groups', 'seq')), parts along dimension 0
- cross_out: bfloat16 [4096, 5120], P(('groups', 'seq')), parts along dimension 0
The draws below stay inside these ranges and needn't reach their ends.
There are 2 independent parts, one for each index of `groups`. The reference program is written for one: setup_inputs(seed, part) draws one part's arguments, and reference() takes and returns one part's arrays. A program takes and returns all parts, laid end to end along the dimension named above; an argument that names none is the same for every part. Nothing has to cross between parts.
All inputs are finite; a program needn't handle non-finite values.
Results may differ from the reference program's by a relative error of at most 0.006.
The reference program's roundings to bfloat16 on the way count: a program that leaves them out, or rounds other values in their place, can miss the bound.
Values may be sent and summed in bfloat16 or wider, within the bound.
A program may use at most 128 MiB of HBM per device.

```python
import math
import jax
import jax.numpy as jnp
from jax import lax

H = 40
HD = 128
CTX = 4096
D = 5120
TXT = 256
TOK_DEV = 128
SB = 16
TOKENS = 2048


def scaled_rows(key, row_count, col_count):
    noise_key = jax.random.fold_in(key, 0)
    values = jnp.clip(jax.random.normal(noise_key, (row_count, col_count), jnp.float32), -4.0, 4.0)
    return values


def draw_self_query(key, part):
    return scaled_rows(jax.random.fold_in(key, 11), TOKENS, D).astype(jnp.bfloat16)


def draw_self_key(key, part):
    return scaled_rows(jax.random.fold_in(key, 12), TOKENS, D).astype(jnp.bfloat16)


def draw_cross_query(key, part):
    return scaled_rows(jax.random.fold_in(key, 13), TOKENS, D).astype(jnp.bfloat16)


def touch_ends(entries, own_key, low, top_value):
    extent = entries.shape
    index_at = [jax.random.randint(jax.random.fold_in(own_key, axis), (), 0, extent[axis]) for axis in range(len(extent))]
    entries = entries.at[tuple(index_at)].set(low)
    longest = extent.index(max(extent))
    index_at[longest] = (index_at[longest] + 1) % extent[longest]
    return entries.at[tuple(index_at)].set(top_value)


def steps_of(rng, shape, pieces, low, high):
    loudness = 1.0
    for dim, shards_of in pieces:
        steps = jax.random.uniform(jax.random.fold_in(jax.random.fold_in(rng, 6), dim), (shards_of,), jnp.float32, low / len(pieces), high / len(pieces))
        loudness = loudness * jnp.repeat(jnp.exp(steps), shape[dim] // shards_of).reshape((-1,) + (1,) * (len(shape) - 1 - dim))
    return loudness


def normal_values(key, extent, scale, most, shards=(), kind=jnp.bfloat16):
    level = steps_of(key, extent, shards, -0.22, 0.18) if shards else 1.0
    entries = jax.random.normal(key, extent, jnp.float32) * scale * level
    return jnp.minimum(jnp.maximum(entries, -most), most).astype(kind)


def setup_inputs(seed: int = 0, part: int = 0) -> dict:
    key_list = jax.random.split(jax.random.key(seed), 9)
    part_splits = jax.random.split(jax.random.fold_in(key_list[8], part), 9)
    return {
        "self_query": draw_self_query(jax.random.fold_in(jax.random.fold_in(key_list[8], part), 71), part),
        "self_key": draw_self_key(jax.random.fold_in(jax.random.fold_in(key_list[8], part), 71), part),
        "self_value": normal_values(part_splits[2], (TOKENS, D), 1.0, 6.0, ((0, 16),)),
        "cross_query": draw_cross_query(jax.random.fold_in(jax.random.fold_in(key_list[8], part), 71), part),
        "context": normal_values(part_splits[4], (TXT, CTX), 1.0, 6.0),
        "key_weight": normal_values(key_list[5], (CTX, D), CTX ** -0.5, 0.09375, ((1, 16),)),
        "value_weight": normal_values(key_list[6], (CTX, D), CTX ** -0.5, 0.09375, ((1, 16),)),
        "band_width": touch_ends(jax.random.randint(key_list[7], (H,), 0, SB), jax.random.fold_in(key_list[7], 1), 0, SB - 1).astype(jnp.int32),
    }


def reference(self_query, self_key, self_value, cross_query, context, key_weight, value_weight, band_width):
    softmax_scale = 1.0 / math.sqrt(HD)
    stripe_len = SB * TOK_DEV
    stripe_count = TOKENS // stripe_len

    def heads_major(source):
        return source.reshape(stripe_count, stripe_len, H, HD).transpose(2, 0, 1, 3)
    block_ids = jnp.arange(stripe_len, dtype=jnp.int32) // TOK_DEV
    block_gap = jnp.abs(block_ids[:, None] - block_ids[None, :])

    def self_head(inputs):
        head_query, head_key, head_value, head_band = inputs
        scores = jnp.einsum('nqd,nkd->nqk', head_query.astype(jnp.float32), head_key.astype(jnp.float32)) * softmax_scale
        allowed = (block_gap <= head_band)[None]
        scores = jnp.where(allowed, scores, -jnp.inf)
        row_max = lax.optimization_barrier(jnp.max(scores, axis=-1, keepdims=True))
        weights = jnp.exp(scores - row_max)
        row_sum = lax.optimization_barrier(jnp.sum(weights, axis=-1, keepdims=True))
        attended = jnp.einsum('nqk,nkd->nqd', weights.astype(jnp.bfloat16).astype(jnp.float32), head_value.astype(jnp.float32))
        return (attended / row_sum).astype(jnp.bfloat16)
    self_heads = lax.map(self_head, (heads_major(self_query), heads_major(self_key), heads_major(self_value), band_width))
    self_out = self_heads.transpose(1, 2, 0, 3).reshape(TOKENS, H * HD)
    text_key = jnp.dot(context, key_weight, preferred_element_type=jnp.float32).astype(jnp.bfloat16)
    text_value = jnp.dot(context, value_weight, preferred_element_type=jnp.float32).astype(jnp.bfloat16)
    text_keys = text_key.reshape(TXT, H, HD).transpose(1, 0, 2)
    text_values = text_value.reshape(TXT, H, HD).transpose(1, 0, 2)
    cross_heads_in = cross_query.reshape(TOKENS, H, HD).transpose(1, 0, 2)

    def cross_head(inputs):
        head_query, head_key, head_value = inputs
        scores = jnp.dot(head_query, head_key.T, preferred_element_type=jnp.float32) * softmax_scale
        row_max = lax.optimization_barrier(jnp.max(scores, axis=-1, keepdims=True))
        weights = jnp.exp(scores - row_max)
        row_sum = lax.optimization_barrier(jnp.sum(weights, axis=-1, keepdims=True))
        attended = jnp.dot(weights.astype(jnp.bfloat16), head_value, preferred_element_type=jnp.float32)
        return (attended / row_sum).astype(jnp.bfloat16)
    cross_heads = lax.map(cross_head, (cross_heads_in, text_keys, text_values))
    cross_out = cross_heads.transpose(1, 0, 2).reshape(TOKENS, H * HD)
    return (self_out, cross_out)
```

```python
import functools
import math

import jax
import jax.numpy as jnp
from jax import lax
from jax.experimental import pallas as pl
from jax.experimental.pallas import tpu as pltpu
from jax.sharding import PartitionSpec as P

SB = 16
PLANE = 4
NT = (((1,), (1,)), ((), ()))
MESH = pl.DeviceIdType.MESH


def kernel(
    devices,
    scale,
    band_ref,
    query_ref,
    key_ref,
    value_ref,
    cross_ref,
    context_ref,
    key_weight_ref,
    value_weight_ref,
    self_out_ref,
    cross_out_ref,
    held,
    attended,
    text,
    context_buf,
    weight_buf,
    load_sem,
    send_sem,
    edge_sem,
    recv_sem,
    back_send_sem,
    back_recv_sem,
    text_send_sem,
    text_recv_sem,
):
    heads = band_ref.shape[0]
    rows = query_ref.shape[0]
    dim = query_ref.shape[1] // heads
    text_cols = key_weight_ref.shape[1]
    device = lax.axis_index("seq")
    me = device % SB
    stripe = device - me
    full = heads // SB
    rest = heads - full * SB
    stride = SB // rest if rest else 1
    sources = (query_ref, key_ref, value_ref)

    def head_cols(head):
        return pl.ds(pl.multiple_of(head * dim, dim), dim)

    def block_rows(index):
        return pl.ds(pl.multiple_of(index * rows, rows), rows)

    loads = [
        pltpu.make_async_copy(source, target, load_sem.at[index])
        for index, (source, target) in enumerate(
            (
                (context_ref, context_buf),
                (key_weight_ref, weight_buf.at[0]),
                (value_weight_ref, weight_buf.at[1]),
            )
        )
    ]
    for load in loads:
        load.start()

    plane = device // PLANE
    place = device % PLANE
    planes = devices // PLANE
    across = plane * PLANE + (1 - place // 2) * 2 + place % 2
    beside = plane * PLANE + (place // 2) * 2 + (1 - place % 2)

    barrier = pltpu.get_barrier_semaphore()

    def greet(step, carry):
        peer = stripe + (me + step) % SB
        pl.semaphore_signal(barrier, inc=1, device_id={"seq": peer}, device_id_type=MESH)
        return carry

    lax.fori_loop(1, SB, greet, 0)

    def greet_plane(step, carry):
        peer_plane = (plane + step) % planes

        @pl.when(peer_plane // (SB // PLANE) != device // SB)
        def _():
            peer = peer_plane * PLANE + place
            pl.semaphore_signal(barrier, inc=1, device_id={"seq": peer}, device_id_type=MESH)

        return carry

    lax.fori_loop(1, planes, greet_plane, 0)
    pl.semaphore_wait(barrier, SB - 1 + planes - SB // PLANE)

    def send_head(slot, head, peer, sem):
        for index, source in enumerate(sources):
            pltpu.make_async_remote_copy(
                src_ref=source.at[:, head_cols(head)],
                dst_ref=held.at[slot, index, block_rows(me), :],
                send_sem=sem,
                recv_sem=recv_sem.at[slot],
                device_id={"seq": stripe + peer},
                device_id_type=MESH,
            ).start()

    def keep_head(slot, head):
        for index, source in enumerate(sources):
            pltpu.make_async_copy(
                source.at[:, head_cols(head)],
                held.at[slot, index, block_rows(me), :],
                recv_sem.at[slot],
            ).start()

    for slot in range(full):

        def send_full(step, carry, slot=slot):
            peer = (me + step) % SB
            send_head(slot, slot * SB + peer, peer, send_sem.at[slot])
            return carry

        lax.fori_loop(1, SB, send_full, 0)
        keep_head(slot, slot * SB + me)

        if slot == 0:
            for load in loads:
                load.wait()
            for index in range(2):
                depth = context_buf.shape[1] // 8

                def project(step, total, index=index, depth=depth):
                    part = pl.ds(pl.multiple_of(step * depth, depth), depth)
                    return total + jnp.dot(
                        context_buf[:, part],
                        weight_buf[index, part, :],
                        preferred_element_type=jnp.float32,
                    )

                total = lax.fori_loop(
                    0, 8, project, jnp.zeros((context_buf.shape[0], text_cols), jnp.float32)
                )
                own = pl.ds(pl.multiple_of(device * text_cols, text_cols), text_cols)
                text[index, own, :] = total.T.astype(jnp.bfloat16)

            def send_text(step, carry):
                peer = ((plane + step) % planes) * PLANE + place
                piece = pl.ds(pl.multiple_of(device * text_cols, text_cols), text_cols)
                pltpu.make_async_remote_copy(
                    src_ref=text.at[:, piece, :],
                    dst_ref=text.at[:, piece, :],
                    send_sem=text_send_sem.at[0],
                    recv_sem=text_recv_sem.at[0],
                    device_id={"seq": peer},
                    device_id_type=MESH,
                ).start()
                return carry

            lax.fori_loop(1, planes, send_text, 0)

    if rest:
        mine = (me % stride == 0) & (me // stride < rest)
        base = me // stride

        def send_rest(step, carry):
            index = (base + step) % rest
            send_head(full, full * SB + index, index * stride, send_sem.at[full])
            return carry

        lax.fori_loop(1, rest, send_rest, 0)
        first = base % rest

        @pl.when(mine)
        def _():
            keep_head(full, full * SB + first)

        @pl.when(jnp.logical_not(mine))
        def _():
            send_head(full, full * SB + first, first * stride, edge_sem)

    def forward_text(phase, peer, places):
        for at in places:

            def forward(step, carry, at=at):
                owner = step * PLANE + at
                piece = pl.ds(pl.multiple_of(owner * text_cols, text_cols), text_cols)
                pltpu.make_async_remote_copy(
                    src_ref=text.at[:, piece, :],
                    dst_ref=text.at[:, piece, :],
                    send_sem=text_send_sem.at[phase],
                    recv_sem=text_recv_sem.at[phase],
                    device_id={"seq": peer},
                    device_id_type=MESH,
                ).start()
                return carry

            lax.fori_loop(0, planes, forward, 0)

    def wait_text(sem, count):
        whole = text.at[:, pl.ds(0, count * text_cols), :]
        pltpu.make_async_copy(whole, whole, sem).wait()

    stripe_len = held.shape[2]
    tile = 2 * rows

    def attend(slot, head):
        band = band_ref[head]
        block_ids = lax.broadcasted_iota(jnp.int32, (1, stripe_len), 1) // rows

        def attend_tile(step, carry):
            at = pl.ds(pl.multiple_of(step * tile, tile), tile)
            scores = lax.dot_general(
                held[slot, 0, at, :], held[slot, 1], NT, preferred_element_type=jnp.float32
            )
            for half in range(2):
                gap = jnp.abs(block_ids - (2 * step + half))
                mask = jnp.where(gap <= band, 0.0, -jnp.inf)
                part = scores[half * rows : (half + 1) * rows] + mask
                top = jnp.max(part, axis=1, keepdims=True)
                weights = jnp.exp2((part - top) * (scale * math.log2(math.e)))
                total = jnp.sum(weights, axis=1, keepdims=True)
                summed = jnp.dot(
                    weights.astype(jnp.bfloat16),
                    held[slot, 2],
                    preferred_element_type=jnp.float32,
                )
                attended[slot, block_rows(2 * step + half), :] = (summed / total).astype(
                    jnp.bfloat16
                )
            return carry

        lax.fori_loop(0, stripe_len // tile, attend_tile, 0)

    def give_back(slot, head):
        def give(step, carry):
            peer = (me + step) % SB
            pltpu.make_async_remote_copy(
                src_ref=attended.at[slot, block_rows(peer), :],
                dst_ref=self_out_ref.at[:, head_cols(head)],
                send_sem=back_send_sem.at[slot],
                recv_sem=back_recv_sem,
                device_id={"seq": stripe + peer},
                device_id_type=MESH,
            ).start()
            return carry

        lax.fori_loop(1, SB, give, 0)
        pltpu.make_async_copy(
            attended.at[slot, block_rows(me), :],
            self_out_ref.at[:, head_cols(head)],
            back_recv_sem,
        ).start()

    def wait_held(slot):
        pltpu.make_async_copy(held.at[slot], held.at[slot], recv_sem.at[slot]).wait()

    def cross():
        def cross_head(head, carry):
            at = pl.ds(pl.multiple_of(head * dim, dim), dim)
            scores = jnp.dot(
                cross_ref[:, at], text[0, at, :], preferred_element_type=jnp.float32
            )
            top = jnp.max(scores, axis=1, keepdims=True)
            weights = jnp.exp2((scores - top) * (scale * math.log2(math.e)))
            total = jnp.sum(weights, axis=1, keepdims=True)
            summed = lax.dot_general(
                weights.astype(jnp.bfloat16), text[1, at, :], NT, preferred_element_type=jnp.float32
            )
            cross_out_ref[:, at] = (summed / total).astype(jnp.bfloat16)
            return carry

        lax.fori_loop(0, heads, cross_head, 0, unroll=4 if heads % 4 == 0 else 1)

    wait_text(text_recv_sem.at[0], planes - 1)
    forward_text(1, across, (place,))
    wait_held(0)
    attend(0, me)
    give_back(0, me)
    wait_text(text_recv_sem.at[1], planes)
    forward_text(2, beside, (place, (1 - place // 2) * 2 + place % 2))
    for slot in range(1, full):
        wait_held(slot)
        attend(slot, slot * SB + me)
        give_back(slot, slot * SB + me)
    wait_text(text_recv_sem.at[2], 2 * planes)
    cross()
    if rest:

        @pl.when(mine)
        def _():
            wait_held(full)
            attend(full, full * SB + first)
            give_back(full, full * SB + first)
            done = attended.at[full, pl.ds(0, (SB - 1) * rows), :]
            pltpu.make_async_copy(done, done, back_send_sem.at[full]).wait()

        @pl.when(jnp.logical_not(mine))
        def _():
            sent = held.at[full, :, pl.ds(0, rows), :]
            pltpu.make_async_copy(sent, sent, edge_sem).wait()

        sent = held.at[full, :, pl.ds(0, (rest - 1) * rows), :]
        pltpu.make_async_copy(sent, sent, send_sem.at[full]).wait()

    for slot in range(full):
        sent = held.at[slot, :, pl.ds(0, (SB - 1) * rows), :]
        pltpu.make_async_copy(sent, sent, send_sem.at[slot]).wait()
        done = attended.at[slot, pl.ds(0, (SB - 1) * rows), :]
        pltpu.make_async_copy(done, done, back_send_sem.at[slot]).wait()
    wait_text(text_send_sem.at[0], planes - 1)
    wait_text(text_send_sem.at[1], planes)
    wait_text(text_send_sem.at[2], 2 * planes)
    pltpu.make_async_copy(self_out_ref, self_out_ref, back_recv_sem).wait()


def shards(
    self_query, self_key, self_value, cross_query, context, key_weight, value_weight, band_width
):
    devices = lax.axis_size("seq")
    rows, width = self_query.shape
    heads = band_width.shape[0]
    dim = width // heads
    slots = (heads + SB - 1) // SB
    text_len, depth = context.shape
    text_cols = key_weight.shape[1]
    vmem = pl.BlockSpec(memory_space=pltpu.VMEM)
    hbm = pl.BlockSpec(memory_space=pl.ANY)
    dtype = jnp.bfloat16
    return pl.pallas_call(
        functools.partial(kernel, devices, 1.0 / math.sqrt(dim)),
        out_shape=(
            jax.ShapeDtypeStruct((rows, width), dtype),
            jax.ShapeDtypeStruct((rows, width), dtype),
        ),
        in_specs=[
            pl.BlockSpec(memory_space=pltpu.SMEM),
            hbm,
            hbm,
            hbm,
            vmem,
            hbm,
            hbm,
            hbm,
        ],
        out_specs=(vmem, vmem),
        scratch_shapes=[
            pltpu.VMEM((slots, 3, SB * rows, dim), dtype),
            pltpu.VMEM((slots, SB * rows, dim), dtype),
            pltpu.VMEM((2, width, text_len), dtype),
            pltpu.VMEM((text_len, depth), dtype),
            pltpu.VMEM((2, depth, text_cols), dtype),
            pltpu.SemaphoreType.DMA((3,)),
            pltpu.SemaphoreType.DMA((slots,)),
            pltpu.SemaphoreType.DMA,
            pltpu.SemaphoreType.DMA((slots,)),
            pltpu.SemaphoreType.DMA((slots,)),
            pltpu.SemaphoreType.DMA,
            pltpu.SemaphoreType.DMA((3,)),
            pltpu.SemaphoreType.DMA((3,)),
        ],
        compiler_params=pltpu.CompilerParams(
            collective_id=0, has_side_effects=True, vmem_limit_bytes=56 * 1024 * 1024
        ),
        cost_estimate=pl.CostEstimate(
            flops=4 * slots * (SB * rows) ** 2 * dim,
            bytes_accessed=16 * rows * width,
            transcendentals=slots * (SB * rows) ** 2,
        ),
    )(
        band_width,
        self_query,
        self_key,
        self_value,
        cross_query,
        context,
        key_weight,
        value_weight,
    )


def solution(mesh):
    in_specs = (
        P(("groups", "seq"), None),
        P(("groups", "seq"), None),
        P(("groups", "seq"), None),
        P(("groups", "seq"), None),
        P("groups", None),
        P(None, "seq"),
        P(None, "seq"),
        P(),
    )
    out_specs = (P(("groups", "seq"), None), P(("groups", "seq"), None))
    return jax.shard_map(shards, mesh=mesh, in_specs=in_specs, out_specs=out_specs, check_vma=False)
```

```python
import functools
import math

import jax
import jax.numpy as jnp
from jax import lax
from jax.experimental import pallas as pl
from jax.experimental.pallas import tpu as pltpu
from jax.sharding import PartitionSpec as P

SB = 16
PLANE = 4
NT = (((1,), (1,)), ((), ()))
MESH = pl.DeviceIdType.MESH


def kernel(
    devices,
    scale,
    band_ref,
    query_ref,
    key_ref,
    value_ref,
    cross_ref,
    context_ref,
    key_weight_ref,
    value_weight_ref,
    self_out_ref,
    cross_out_ref,
    held,
    attended,
    text,
    context_buf,
    weight_buf,
    load_sem,
    send_sem,
    edge_sem,
    recv_sem,
    back_send_sem,
    back_recv_sem,
    text_send_sem,
    text_recv_sem,
    pass_send_sem,
    pass_recv_sem,
):
    heads = band_ref.shape[0]
    rows = query_ref.shape[0]
    dim = query_ref.shape[1] // heads
    text_cols = key_weight_ref.shape[0]
    device = lax.axis_index("seq")
    me = device % SB
    stripe = device - me
    full = heads // SB
    rest = heads - full * SB
    stride = SB // rest if rest else 1
    sources = (query_ref, key_ref, value_ref)

    def head_cols(head):
        return pl.ds(pl.multiple_of(head * dim, dim), dim)

    def block_rows(index):
        return pl.ds(pl.multiple_of(index * rows, rows), rows)

    loads = [
        pltpu.make_async_copy(source, target, load_sem.at[index])
        for index, (source, target) in enumerate(
            (
                (context_ref, context_buf),
                (key_weight_ref, weight_buf.at[0]),
                (value_weight_ref, weight_buf.at[1]),
            )
        )
    ]
    for load in loads:
        load.start()

    plane = device // PLANE
    place = device % PLANE
    planes = devices // PLANE
    across = plane * PLANE + (1 - place // 2) * 2 + place % 2
    beside = plane * PLANE + (place // 2) * 2 + (1 - place % 2)

    barrier = pltpu.get_barrier_semaphore()

    def greet(step, carry):
        peer = stripe + (me + step) % SB
        pl.semaphore_signal(barrier, inc=1, device_id={"seq": peer}, device_id_type=MESH)
        return carry

    lax.fori_loop(1, SB, greet, 0)

    pl.semaphore_wait(barrier, SB - 1)
    for side in (-1, 1):
        next_plane = plane + side

        @pl.when(
            (next_plane >= 0)
            & (next_plane < planes)
            & ((next_plane + planes) // (SB // PLANE) != (plane + planes) // (SB // PLANE))
        )
        def _(next_plane=next_plane):
            peer = next_plane * PLANE + place
            pl.semaphore_signal(barrier, inc=1, device_id={"seq": peer}, device_id_type=MESH)
            pl.semaphore_wait(barrier, 1)


    def send_head(slot, head, peer, sem):
        for index, source in enumerate(sources):
            pltpu.make_async_remote_copy(
                src_ref=source.at[:, head_cols(head)],
                dst_ref=held.at[slot, index, block_rows(me), :],
                send_sem=sem,
                recv_sem=recv_sem.at[slot],
                device_id={"seq": stripe + peer},
                device_id_type=MESH,
            ).start()

    def keep_head(slot, head):
        for index, source in enumerate(sources):
            pltpu.make_async_copy(
                source.at[:, head_cols(head)],
                held.at[slot, index, block_rows(me), :],
                recv_sem.at[slot],
            ).start()

    def send_full(slot, low, high):
        def send(step, carry):
            peer = (me + step) % SB
            send_head(slot, slot * SB + peer, peer, send_sem.at[slot])
            return carry

        lax.fori_loop(low, high, send, 0)

    def text_piece(owner):
        return text.at[:, pl.ds(pl.multiple_of(owner * text_cols, text_cols), text_cols), :]

    def pass_text(hop, side, act):
        come_from = plane - side * hop
        go_to = plane + side

        @pl.when((come_from >= 0) & (come_from < planes) & (go_to >= 0) & (go_to < planes))
        def _():
            piece = text_piece(come_from * PLANE + place)
            way = (side + 1) // 2
            copy = pltpu.make_async_remote_copy(
                src_ref=piece,
                dst_ref=piece,
                send_sem=pass_send_sem.at[way, hop],
                recv_sem=pass_recv_sem.at[way, hop],
                device_id={"seq": go_to * PLANE + place},
                device_id_type=MESH,
            )
            if act == "start":
                copy.start()
            else:
                copy.wait_send()

    def take_text(hop, side):
        come_from = plane - side * (hop + 1)

        @pl.when((come_from >= 0) & (come_from < planes))
        def _():
            piece = text_piece(come_from * PLANE + place)
            pltpu.make_async_copy(piece, piece, pass_recv_sem.at[(side + 1) // 2, hop]).wait()

    cuts = [1 + (SB - 1) * part // planes for part in range(planes + 1)]
    send_full(0, cuts[0], cuts[1])
    keep_head(0, me)
    for load in loads:
        load.wait()
    for index in range(2):
        depth = context_buf.shape[1] // 8

        def project(step, total, index=index, depth=depth):
            part = pl.ds(pl.multiple_of(step * depth, depth), depth)
            return total + lax.dot_general(
                weight_buf[index, :, part],
                context_buf[:, part],
                NT,
                preferred_element_type=jnp.float32,
            )

        total = lax.fori_loop(
            0, 8, project, jnp.zeros((text_cols, context_buf.shape[0]), jnp.float32)
        )
        own = pl.ds(pl.multiple_of(device * text_cols, text_cols), text_cols)
        text[index, own, :] = total.astype(jnp.bfloat16)
    for hop in range(planes - 1):
        if hop:
            for side in (-1, 1):
                take_text(hop - 1, side)
        for side in (-1, 1):
            pass_text(hop, side, "start")
        send_full(0, cuts[hop + 1], cuts[hop + 2])
    for slot in range(1, full):
        send_full(slot, 1, SB)
        keep_head(slot, slot * SB + me)

    if rest:
        mine = (me % stride == 0) & (me // stride < rest)
        base = me // stride

        def send_rest(step, carry):
            index = (base + step) % rest
            send_head(full, full * SB + index, index * stride, send_sem.at[full])
            return carry

        lax.fori_loop(1, rest, send_rest, 0)
        first = base % rest

        @pl.when(mine)
        def _():
            keep_head(full, full * SB + first)

        @pl.when(jnp.logical_not(mine))
        def _():
            send_head(full, full * SB + first, first * stride, edge_sem)

    def forward_text(phase, peer, places):
        for at in places:

            def forward(step, carry, at=at):
                piece = text_piece(step * PLANE + at)
                pltpu.make_async_remote_copy(
                    src_ref=piece,
                    dst_ref=piece,
                    send_sem=text_send_sem.at[phase],
                    recv_sem=text_recv_sem.at[phase],
                    device_id={"seq": peer},
                    device_id_type=MESH,
                ).start()
                return carry

            lax.fori_loop(0, planes, forward, 0)

    def wait_text(sem, count):
        whole = text.at[:, pl.ds(0, count * text_cols), :]
        pltpu.make_async_copy(whole, whole, sem).wait()

    stripe_len = held.shape[2]
    tile = 2 * rows

    def attend(slot, head):
        band = band_ref[head]
        block_ids = lax.broadcasted_iota(jnp.int32, (1, stripe_len), 1) // rows

        def attend_tile(step, carry):
            at = pl.ds(pl.multiple_of(step * tile, tile), tile)
            scores = lax.dot_general(
                held[slot, 0, at, :], held[slot, 1], NT, preferred_element_type=jnp.float32
            )
            for half in range(2):
                gap = jnp.abs(block_ids - (2 * step + half))
                mask = jnp.where(gap <= band, 0.0, -jnp.inf)
                part = scores[half * rows : (half + 1) * rows] + mask
                top = jnp.max(part, axis=1, keepdims=True)
                weights = jnp.exp2((part - top) * (scale * math.log2(math.e)))
                total = jnp.sum(weights, axis=1, keepdims=True)
                summed = jnp.dot(
                    weights.astype(jnp.bfloat16),
                    held[slot, 2],
                    preferred_element_type=jnp.float32,
                )
                attended[slot, block_rows(2 * step + half), :] = (summed / total).astype(
                    jnp.bfloat16
                )
            return carry

        lax.fori_loop(0, stripe_len // tile, attend_tile, 0)

    def give_back(slot, head):
        def give(step, carry):
            peer = (me + step) % SB
            pltpu.make_async_remote_copy(
                src_ref=attended.at[slot, block_rows(peer), :],
                dst_ref=self_out_ref.at[:, head_cols(head)],
                send_sem=back_send_sem.at[slot],
                recv_sem=back_recv_sem,
                device_id={"seq": stripe + peer},
                device_id_type=MESH,
            ).start()
            return carry

        lax.fori_loop(1, SB, give, 0)
        pltpu.make_async_copy(
            attended.at[slot, block_rows(me), :],
            self_out_ref.at[:, head_cols(head)],
            back_recv_sem,
        ).start()

    def wait_held(slot):
        pltpu.make_async_copy(held.at[slot], held.at[slot], recv_sem.at[slot]).wait()

    def cross():
        def cross_head(head, carry):
            at = pl.ds(pl.multiple_of(head * dim, dim), dim)
            scores = jnp.dot(
                cross_ref[:, at], text[0, at, :], preferred_element_type=jnp.float32
            )
            top = jnp.max(scores, axis=1, keepdims=True)
            weights = jnp.exp2((scores - top) * (scale * math.log2(math.e)))
            total = jnp.sum(weights, axis=1, keepdims=True)
            summed = lax.dot_general(
                weights.astype(jnp.bfloat16), text[1, at, :], NT, preferred_element_type=jnp.float32
            )
            cross_out_ref[:, at] = (summed / total).astype(jnp.bfloat16)
            return carry

        lax.fori_loop(0, heads, cross_head, 0, unroll=4 if heads % 4 == 0 else 1)

    for side in (-1, 1):
        take_text(planes - 2, side)
    forward_text(0, across, (place,))
    wait_held(0)
    attend(0, me)
    give_back(0, me)
    wait_text(text_recv_sem.at[0], planes)
    forward_text(1, beside, (place, (1 - place // 2) * 2 + place % 2))
    for slot in range(1, full):
        wait_held(slot)
        attend(slot, slot * SB + me)
        give_back(slot, slot * SB + me)
    wait_text(text_recv_sem.at[1], 2 * planes)
    cross()
    if rest:

        @pl.when(mine)
        def _():
            wait_held(full)
            attend(full, full * SB + first)
            give_back(full, full * SB + first)
            done = attended.at[full, pl.ds(0, (SB - 1) * rows), :]
            pltpu.make_async_copy(done, done, back_send_sem.at[full]).wait()

        @pl.when(jnp.logical_not(mine))
        def _():
            sent = held.at[full, :, pl.ds(0, rows), :]
            pltpu.make_async_copy(sent, sent, edge_sem).wait()

        sent = held.at[full, :, pl.ds(0, (rest - 1) * rows), :]
        pltpu.make_async_copy(sent, sent, send_sem.at[full]).wait()

    for slot in range(full):
        sent = held.at[slot, :, pl.ds(0, (SB - 1) * rows), :]
        pltpu.make_async_copy(sent, sent, send_sem.at[slot]).wait()
        done = attended.at[slot, pl.ds(0, (SB - 1) * rows), :]
        pltpu.make_async_copy(done, done, back_send_sem.at[slot]).wait()
    for hop in range(planes - 1):
        for side in (-1, 1):
            pass_text(hop, side, "wait")
    wait_text(text_send_sem.at[0], planes)
    wait_text(text_send_sem.at[1], 2 * planes)
    pltpu.make_async_copy(self_out_ref, self_out_ref, back_recv_sem).wait()


def shards(
    self_query, self_key, self_value, cross_query, context, key_weight, value_weight, band_width
):
    devices = lax.axis_size("seq")
    rows, width = self_query.shape
    heads = band_width.shape[0]
    dim = width // heads
    slots = (heads + SB - 1) // SB
    text_len, depth = context.shape
    text_cols = key_weight.shape[1]
    vmem = pl.BlockSpec(memory_space=pltpu.VMEM)
    hbm = pl.BlockSpec(memory_space=pl.ANY)
    dtype = jnp.bfloat16
    return pl.pallas_call(
        functools.partial(kernel, devices, 1.0 / math.sqrt(dim)),
        out_shape=(
            jax.ShapeDtypeStruct((rows, width), dtype),
            jax.ShapeDtypeStruct((rows, width), dtype),
        ),
        in_specs=[
            pl.BlockSpec(memory_space=pltpu.SMEM),
            hbm,
            hbm,
            hbm,
            vmem,
            hbm,
            hbm,
            hbm,
        ],
        out_specs=(vmem, vmem),
        scratch_shapes=[
            pltpu.VMEM((slots, 3, SB * rows, dim), dtype),
            pltpu.VMEM((slots, SB * rows, dim), dtype),
            pltpu.VMEM((2, width, text_len), dtype),
            pltpu.VMEM((text_len, depth), dtype),
            pltpu.VMEM((2, text_cols, depth), dtype),
            pltpu.SemaphoreType.DMA((3,)),
            pltpu.SemaphoreType.DMA((slots,)),
            pltpu.SemaphoreType.DMA,
            pltpu.SemaphoreType.DMA((slots,)),
            pltpu.SemaphoreType.DMA((slots,)),
            pltpu.SemaphoreType.DMA,
            pltpu.SemaphoreType.DMA((2,)),
            pltpu.SemaphoreType.DMA((2,)),
            pltpu.SemaphoreType.DMA((2, devices // PLANE)),
            pltpu.SemaphoreType.DMA((2, devices // PLANE)),
        ],
        compiler_params=pltpu.CompilerParams(
            collective_id=0, has_side_effects=True, vmem_limit_bytes=56 * 1024 * 1024
        ),
        cost_estimate=pl.CostEstimate(
            flops=4 * slots * (SB * rows) ** 2 * dim,
            bytes_accessed=16 * rows * width,
            transcendentals=slots * (SB * rows) ** 2,
        ),
    )(
        band_width,
        self_query,
        self_key,
        self_value,
        cross_query,
        context,
        key_weight.T,
        value_weight.T,
    )


def solution(mesh):
    in_specs = (
        P(("groups", "seq"), None),
        P(("groups", "seq"), None),
        P(("groups", "seq"), None),
        P(("groups", "seq"), None),
        P("groups", None),
        P(None, "seq"),
        P(None, "seq"),
        P(),
    )
    out_specs = (P(("groups", "seq"), None), P(("groups", "seq"), None))
    return jax.shard_map(shards, mesh=mesh, in_specs=in_specs, out_specs=out_specs, check_vma=False)
```

```python
import functools
import math

import jax
import jax.numpy as jnp
from jax import lax
from jax.experimental import pallas as pl
from jax.experimental.pallas import tpu as pltpu
from jax.sharding import PartitionSpec as P

SB = 16
PLANE = 4
NT = (((1,), (1,)), ((), ()))
MESH = pl.DeviceIdType.MESH


def kernel(
    devices,
    scale,
    band_ref,
    query_ref,
    key_ref,
    value_ref,
    cross_ref,
    context_ref,
    key_weight_ref,
    value_weight_ref,
    self_out_ref,
    cross_out_ref,
    held,
    attended,
    text,
    context_buf,
    weight_buf,
    load_sem,
    send_sem,
    edge_sem,
    recv_sem,
    back_send_sem,
    back_recv_sem,
    text_send_sem,
    text_recv_sem,
    pass_send_sem,
    pass_recv_sem,
    scores,
    weights,
    totals,
    summed,
):
    heads = band_ref.shape[0]
    rows = query_ref.shape[0]
    dim = query_ref.shape[1] // heads
    text_cols = key_weight_ref.shape[0]
    device = lax.axis_index("seq")
    me = device % SB
    stripe = device - me
    full = heads // SB
    rest = heads - full * SB
    stride = SB // rest if rest else 1
    sources = (query_ref, key_ref, value_ref)

    def head_cols(head):
        return pl.ds(pl.multiple_of(head * dim, dim), dim)

    def block_rows(index):
        return pl.ds(pl.multiple_of(index * rows, rows), rows)

    loads = [
        pltpu.make_async_copy(source, target, load_sem.at[index])
        for index, (source, target) in enumerate(
            (
                (context_ref, context_buf),
                (key_weight_ref, weight_buf.at[0]),
                (value_weight_ref, weight_buf.at[1]),
            )
        )
    ]
    for load in loads:
        load.start()

    plane = device // PLANE
    place = device % PLANE
    planes = devices // PLANE
    across = plane * PLANE + (1 - place // 2) * 2 + place % 2
    beside = plane * PLANE + (place // 2) * 2 + (1 - place % 2)

    barrier = pltpu.get_barrier_semaphore()

    def greet(step, carry):
        peer = stripe + (me + step) % SB
        pl.semaphore_signal(barrier, inc=1, device_id={"seq": peer}, device_id_type=MESH)
        return carry

    lax.fori_loop(1, SB, greet, 0)

    pl.semaphore_wait(barrier, SB - 1)
    for side in (-1, 1):
        next_plane = plane + side

        @pl.when(
            (next_plane >= 0)
            & (next_plane < planes)
            & ((next_plane + planes) // (SB // PLANE) != (plane + planes) // (SB // PLANE))
        )
        def _(next_plane=next_plane):
            peer = next_plane * PLANE + place
            pl.semaphore_signal(barrier, inc=1, device_id={"seq": peer}, device_id_type=MESH)
            pl.semaphore_wait(barrier, 1)


    def send_head(slot, head, peer, sem):
        for index, source in enumerate(sources):
            pltpu.make_async_remote_copy(
                src_ref=source.at[:, head_cols(head)],
                dst_ref=held.at[slot, index, block_rows(me), :],
                send_sem=sem,
                recv_sem=recv_sem.at[slot],
                device_id={"seq": stripe + peer},
                device_id_type=MESH,
            ).start()

    def keep_head(slot, head):
        for index, source in enumerate(sources):
            pltpu.make_async_copy(
                source.at[:, head_cols(head)],
                held.at[slot, index, block_rows(me), :],
                recv_sem.at[slot],
            ).start()

    def send_full(slot, low, high):
        def send(step, carry):
            peer = (me + step) % SB
            send_head(slot, slot * SB + peer, peer, send_sem.at[slot])
            return carry

        lax.fori_loop(low, high, send, 0)

    def text_piece(owner):
        return text.at[:, pl.ds(pl.multiple_of(owner * text_cols, text_cols), text_cols), :]

    def pass_text(hop, side, act):
        come_from = plane - side * hop
        go_to = plane + side

        @pl.when((come_from >= 0) & (come_from < planes) & (go_to >= 0) & (go_to < planes))
        def _():
            piece = text_piece(come_from * PLANE + place)
            way = (side + 1) // 2
            copy = pltpu.make_async_remote_copy(
                src_ref=piece,
                dst_ref=piece,
                send_sem=pass_send_sem.at[way, hop],
                recv_sem=pass_recv_sem.at[way, hop],
                device_id={"seq": go_to * PLANE + place},
                device_id_type=MESH,
            )
            if act == "start":
                copy.start()
            else:
                copy.wait_send()

    def take_text(hop, side):
        come_from = plane - side * (hop + 1)

        @pl.when((come_from >= 0) & (come_from < planes))
        def _():
            piece = text_piece(come_from * PLANE + place)
            pltpu.make_async_copy(piece, piece, pass_recv_sem.at[(side + 1) // 2, hop]).wait()

    cuts = [1 + (SB - 1) * part // planes for part in range(planes + 1)]
    send_full(0, cuts[0], cuts[1])
    keep_head(0, me)
    for load in loads:
        load.wait()
    for index in range(2):
        depth = context_buf.shape[1] // 8

        def project(step, total, index=index, depth=depth):
            part = pl.ds(pl.multiple_of(step * depth, depth), depth)
            return total + lax.dot_general(
                weight_buf[index, :, part],
                context_buf[:, part],
                NT,
                preferred_element_type=jnp.float32,
            )

        total = lax.fori_loop(
            0, 8, project, jnp.zeros((text_cols, context_buf.shape[0]), jnp.float32)
        )
        own = pl.ds(pl.multiple_of(device * text_cols, text_cols), text_cols)
        text[index, own, :] = total.astype(jnp.bfloat16)
    for hop in range(planes - 1):
        if hop:
            for side in (-1, 1):
                take_text(hop - 1, side)
        for side in (-1, 1):
            pass_text(hop, side, "start")
        send_full(0, cuts[hop + 1], cuts[hop + 2])
    for slot in range(1, full):
        send_full(slot, 1, SB)
        keep_head(slot, slot * SB + me)

    if rest:
        mine = (me % stride == 0) & (me // stride < rest)
        base = me // stride

        def send_rest(step, carry):
            index = (base + step) % rest
            send_head(full, full * SB + index, index * stride, send_sem.at[full])
            return carry

        lax.fori_loop(1, rest, send_rest, 0)
        first = base % rest

        @pl.when(mine)
        def _():
            keep_head(full, full * SB + first)

        @pl.when(jnp.logical_not(mine))
        def _():
            send_head(full, full * SB + first, first * stride, edge_sem)

    def forward_text(phase, peer, places):
        for at in places:

            def forward(step, carry, at=at):
                piece = text_piece(step * PLANE + at)
                pltpu.make_async_remote_copy(
                    src_ref=piece,
                    dst_ref=piece,
                    send_sem=text_send_sem.at[phase],
                    recv_sem=text_recv_sem.at[phase],
                    device_id={"seq": peer},
                    device_id_type=MESH,
                ).start()
                return carry

            lax.fori_loop(0, planes, forward, 0)

    def wait_text(sem, count):
        whole = text.at[:, pl.ds(0, count * text_cols), :]
        pltpu.make_async_copy(whole, whole, sem).wait()

    stripe_len = held.shape[2]
    tile = scores.shape[1]
    tiles = stripe_len // tile

    def attend(slot, head):
        band = band_ref[head]
        block_ids = lax.broadcasted_iota(jnp.int32, (1, stripe_len), 1) // rows

        def score(step, part):
            cols = pl.ds(pl.multiple_of(part * tile, tile), tile)
            scores[step % 2, :, cols] = lax.dot_general(
                held[slot, 0, step * tile : (step + 1) * tile, :],
                held[slot, 1, cols, :],
                NT,
                preferred_element_type=jnp.float32,
            )

        def weigh(step, part):
            gap = jnp.abs(block_ids - (step * (tile // rows) + part))
            mask = jnp.where(gap <= band, 0.0, -jnp.inf)
            masked = scores[step % 2, block_rows(part), :] + mask
            top = jnp.max(masked, axis=1, keepdims=True)
            raised = jnp.exp2((masked - top) * (scale * math.log2(math.e)))
            total = jnp.sum(raised, axis=1, keepdims=True)
            totals[step % 2, block_rows(part), :] = jnp.broadcast_to(total, (rows, dim))
            weights[step % 2, block_rows(part), :] = raised.astype(jnp.bfloat16)

        def add_up(step, part):
            cols = pl.ds(pl.multiple_of(part * tile, tile), tile)
            summed[...] += jnp.dot(
                weights[step % 2, :, cols],
                held[slot, 2, cols, :],
                preferred_element_type=jnp.float32,
            )

        for step in range(-1, tiles + 1):

            def stage(part, carry, step=step):
                if step + 1 < tiles:
                    score(step + 1, part)
                if 0 <= step < tiles:
                    weigh(step, part)
                if step >= 1:
                    add_up(step - 1, part)
                return carry

            if step >= 1:
                summed[...] = jnp.zeros_like(summed)
            lax.fori_loop(0, stripe_len // tile, stage, 0)
            if step >= 1:
                attended[slot, (step - 1) * tile : step * tile, :] = (
                    summed[...] / totals[(step - 1) % 2]
                ).astype(jnp.bfloat16)

    def give_back(slot, head):
        def give(step, carry):
            peer = (me + step) % SB
            pltpu.make_async_remote_copy(
                src_ref=attended.at[slot, block_rows(peer), :],
                dst_ref=self_out_ref.at[:, head_cols(head)],
                send_sem=back_send_sem.at[slot],
                recv_sem=back_recv_sem,
                device_id={"seq": stripe + peer},
                device_id_type=MESH,
            ).start()
            return carry

        lax.fori_loop(1, SB, give, 0)
        pltpu.make_async_copy(
            attended.at[slot, block_rows(me), :],
            self_out_ref.at[:, head_cols(head)],
            back_recv_sem,
        ).start()

    def wait_held(slot):
        pltpu.make_async_copy(held.at[slot], held.at[slot], recv_sem.at[slot]).wait()

    def cross():
        def cross_head(head, carry):
            at = pl.ds(pl.multiple_of(head * dim, dim), dim)
            part = jnp.dot(cross_ref[:, at], text[0, at, :], preferred_element_type=jnp.float32)
            top = jnp.max(part, axis=1, keepdims=True)
            raised = jnp.exp2((part - top) * (scale * math.log2(math.e)))
            total = jnp.sum(raised, axis=1, keepdims=True)
            mixed = lax.dot_general(
                raised.astype(jnp.bfloat16), text[1, at, :], NT, preferred_element_type=jnp.float32
            )
            cross_out_ref[:, at] = (mixed / total).astype(jnp.bfloat16)
            return carry

        lax.fori_loop(0, heads, cross_head, 0, unroll=4 if heads % 4 == 0 else 1)

    for side in (-1, 1):
        take_text(planes - 2, side)
    forward_text(0, across, (place,))
    wait_held(0)
    attend(0, me)
    give_back(0, me)
    wait_text(text_recv_sem.at[0], planes)
    forward_text(1, beside, (place, (1 - place // 2) * 2 + place % 2))
    for slot in range(1, full):
        wait_held(slot)
        attend(slot, slot * SB + me)
        give_back(slot, slot * SB + me)
    wait_text(text_recv_sem.at[1], 2 * planes)
    cross()
    if rest:

        @pl.when(mine)
        def _():
            wait_held(full)
            attend(full, full * SB + first)
            give_back(full, full * SB + first)
            done = attended.at[full, pl.ds(0, (SB - 1) * rows), :]
            pltpu.make_async_copy(done, done, back_send_sem.at[full]).wait()

        @pl.when(jnp.logical_not(mine))
        def _():
            sent = held.at[full, :, pl.ds(0, rows), :]
            pltpu.make_async_copy(sent, sent, edge_sem).wait()

        sent = held.at[full, :, pl.ds(0, (rest - 1) * rows), :]
        pltpu.make_async_copy(sent, sent, send_sem.at[full]).wait()

    for slot in range(full):
        sent = held.at[slot, :, pl.ds(0, (SB - 1) * rows), :]
        pltpu.make_async_copy(sent, sent, send_sem.at[slot]).wait()
        done = attended.at[slot, pl.ds(0, (SB - 1) * rows), :]
        pltpu.make_async_copy(done, done, back_send_sem.at[slot]).wait()
    for hop in range(planes - 1):
        for side in (-1, 1):
            pass_text(hop, side, "wait")
    wait_text(text_send_sem.at[0], planes)
    wait_text(text_send_sem.at[1], 2 * planes)
    pltpu.make_async_copy(self_out_ref, self_out_ref, back_recv_sem).wait()


def shards(
    self_query, self_key, self_value, cross_query, context, key_weight, value_weight, band_width
):
    devices = lax.axis_size("seq")
    rows, width = self_query.shape
    heads = band_width.shape[0]
    dim = width // heads
    slots = (heads + SB - 1) // SB
    text_len, depth = context.shape
    text_cols = key_weight.shape[1]
    vmem = pl.BlockSpec(memory_space=pltpu.VMEM)
    hbm = pl.BlockSpec(memory_space=pl.ANY)
    dtype = jnp.bfloat16
    return pl.pallas_call(
        functools.partial(kernel, devices, 1.0 / math.sqrt(dim)),
        out_shape=(
            jax.ShapeDtypeStruct((rows, width), dtype),
            jax.ShapeDtypeStruct((rows, width), dtype),
        ),
        in_specs=[
            pl.BlockSpec(memory_space=pltpu.SMEM),
            hbm,
            hbm,
            hbm,
            vmem,
            hbm,
            hbm,
            hbm,
        ],
        out_specs=(vmem, vmem),
        scratch_shapes=[
            pltpu.VMEM((slots, 3, SB * rows, dim), dtype),
            pltpu.VMEM((slots, SB * rows, dim), dtype),
            pltpu.VMEM((2, width, text_len), dtype),
            pltpu.VMEM((text_len, depth), dtype),
            pltpu.VMEM((2, text_cols, depth), dtype),
            pltpu.SemaphoreType.DMA((3,)),
            pltpu.SemaphoreType.DMA((slots,)),
            pltpu.SemaphoreType.DMA,
            pltpu.SemaphoreType.DMA((slots,)),
            pltpu.SemaphoreType.DMA((slots,)),
            pltpu.SemaphoreType.DMA,
            pltpu.SemaphoreType.DMA((2,)),
            pltpu.SemaphoreType.DMA((2,)),
            pltpu.SemaphoreType.DMA((2, devices // PLANE)),
            pltpu.SemaphoreType.DMA((2, devices // PLANE)),
            pltpu.VMEM((2, PLANE * rows, SB * rows), jnp.float32),
            pltpu.VMEM((2, PLANE * rows, SB * rows), dtype),
            pltpu.VMEM((2, PLANE * rows, dim), jnp.float32),
            pltpu.VMEM((PLANE * rows, dim), jnp.float32),
        ],
        compiler_params=pltpu.CompilerParams(
            collective_id=0, has_side_effects=True, vmem_limit_bytes=56 * 1024 * 1024
        ),
        cost_estimate=pl.CostEstimate(
            flops=4 * slots * (SB * rows) ** 2 * dim,
            bytes_accessed=16 * rows * width,
            transcendentals=slots * (SB * rows) ** 2,
        ),
    )(
        band_width,
        self_query,
        self_key,
        self_value,
        cross_query,
        context,
        key_weight.T,
        value_weight.T,
    )


def solution(mesh):
    in_specs = (
        P(("groups", "seq"), None),
        P(("groups", "seq"), None),
        P(("groups", "seq"), None),
        P(("groups", "seq"), None),
        P("groups", None),
        P(None, "seq"),
        P(None, "seq"),
        P(),
    )
    out_specs = (P(("groups", "seq"), None), P(("groups", "seq"), None))
    return jax.shard_map(shards, mesh=mesh, in_specs=in_specs, out_specs=out_specs, check_vma=False)
```

```python
import functools
import math

import jax
import jax.numpy as jnp
from jax import lax
from jax.experimental import pallas as pl
from jax.experimental.pallas import tpu as pltpu
from jax.sharding import PartitionSpec as P

SB = 16
PLANE = 4
NT = (((1,), (1,)), ((), ()))
MESH = pl.DeviceIdType.MESH


def kernel(
    devices,
    scale,
    band_ref,
    query_ref,
    key_ref,
    value_ref,
    cross_ref,
    context_ref,
    key_weight_ref,
    value_weight_ref,
    self_out_ref,
    cross_out_ref,
    held,
    attended,
    text,
    context_buf,
    weight_buf,
    load_sem,
    send_sem,
    edge_sem,
    recv_sem,
    back_send_sem,
    back_recv_sem,
    text_send_sem,
    text_recv_sem,
    pass_send_sem,
    pass_recv_sem,
):
    heads = band_ref.shape[0]
    rows = query_ref.shape[0]
    dim = query_ref.shape[1] // heads
    text_cols = key_weight_ref.shape[0]
    device = lax.axis_index("seq")
    me = device % SB
    stripe = device - me
    full = heads // SB
    rest = heads - full * SB
    stride = SB // rest if rest else 1
    sources = (query_ref, key_ref, value_ref)

    def head_cols(head):
        return pl.ds(pl.multiple_of(head * dim, dim), dim)

    def block_rows(index):
        return pl.ds(pl.multiple_of(index * rows, rows), rows)

    loads = [
        pltpu.make_async_copy(source, target, load_sem.at[index])
        for index, (source, target) in enumerate(
            (
                (context_ref, context_buf),
                (key_weight_ref, weight_buf.at[0]),
                (value_weight_ref, weight_buf.at[1]),
            )
        )
    ]
    for load in loads:
        load.start()

    plane = device // PLANE
    place = device % PLANE
    planes = devices // PLANE
    across = plane * PLANE + (1 - place // 2) * 2 + place % 2
    beside = plane * PLANE + (place // 2) * 2 + (1 - place % 2)

    barrier = pltpu.get_barrier_semaphore()

    def greet(step, carry):
        peer = stripe + (me + step) % SB
        pl.semaphore_signal(barrier, inc=1, device_id={"seq": peer}, device_id_type=MESH)
        return carry

    lax.fori_loop(1, SB, greet, 0)

    pl.semaphore_wait(barrier, SB - 1)
    for side in (-1, 1):
        next_plane = plane + side

        @pl.when(
            (next_plane >= 0)
            & (next_plane < planes)
            & ((next_plane + planes) // (SB // PLANE) != (plane + planes) // (SB // PLANE))
        )
        def _(next_plane=next_plane):
            peer = next_plane * PLANE + place
            pl.semaphore_signal(barrier, inc=1, device_id={"seq": peer}, device_id_type=MESH)
            pl.semaphore_wait(barrier, 1)


    def send_head(slot, head, peer, sem):
        for index, source in enumerate(sources):
            pltpu.make_async_remote_copy(
                src_ref=source.at[:, head_cols(head)],
                dst_ref=held.at[slot, index, block_rows(me), :],
                send_sem=sem,
                recv_sem=recv_sem.at[slot],
                device_id={"seq": stripe + peer},
                device_id_type=MESH,
            ).start()

    def keep_head(slot, head):
        for index, source in enumerate(sources):
            pltpu.make_async_copy(
                source.at[:, head_cols(head)],
                held.at[slot, index, block_rows(me), :],
                recv_sem.at[slot],
            ).start()

    def send_full(slot, low, high):
        def send(step, carry):
            peer = (me + step) % SB
            send_head(slot, slot * SB + peer, peer, send_sem.at[slot])
            return carry

        lax.fori_loop(low, high, send, 0)

    def text_piece(owner):
        return text.at[:, pl.ds(pl.multiple_of(owner * text_cols, text_cols), text_cols), :]

    def pass_text(hop, side, act):
        come_from = plane - side * hop
        go_to = plane + side

        @pl.when((come_from >= 0) & (come_from < planes) & (go_to >= 0) & (go_to < planes))
        def _():
            piece = text_piece(come_from * PLANE + place)
            way = (side + 1) // 2
            copy = pltpu.make_async_remote_copy(
                src_ref=piece,
                dst_ref=piece,
                send_sem=pass_send_sem.at[way, hop],
                recv_sem=pass_recv_sem.at[way, hop],
                device_id={"seq": go_to * PLANE + place},
                device_id_type=MESH,
            )
            if act == "start":
                copy.start()
            else:
                copy.wait_send()

    def take_text(hop, side):
        come_from = plane - side * (hop + 1)

        @pl.when((come_from >= 0) & (come_from < planes))
        def _():
            piece = text_piece(come_from * PLANE + place)
            pltpu.make_async_copy(piece, piece, pass_recv_sem.at[(side + 1) // 2, hop]).wait()

    cuts = [1 + (SB - 1) * part // planes for part in range(planes + 1)]
    if rest:
        mine = (me % stride == 0) & (me // stride < rest)
        base = me // stride

        def send_rest(step, carry):
            index = (base + step) % rest
            send_head(full, full * SB + index, index * stride, send_sem.at[full])
            return carry

        lax.fori_loop(1, rest, send_rest, 0)
        first = base % rest

        @pl.when(mine)
        def _():
            keep_head(full, full * SB + first)

        @pl.when(jnp.logical_not(mine))
        def _():
            send_head(full, full * SB + first, first * stride, edge_sem)

    send_full(0, cuts[0], cuts[1])
    keep_head(0, me)
    for load in loads:
        load.wait()
    for index in range(2):
        depth = context_buf.shape[1] // 8

        def project(step, total, index=index, depth=depth):
            part = pl.ds(pl.multiple_of(step * depth, depth), depth)
            return total + lax.dot_general(
                weight_buf[index, :, part],
                context_buf[:, part],
                NT,
                preferred_element_type=jnp.float32,
            )

        total = lax.fori_loop(
            0, 8, project, jnp.zeros((text_cols, context_buf.shape[0]), jnp.float32)
        )
        own = pl.ds(pl.multiple_of(device * text_cols, text_cols), text_cols)
        text[index, own, :] = total.astype(jnp.bfloat16)
    for hop in range(planes - 1):
        if hop:
            for side in (-1, 1):
                take_text(hop - 1, side)
        for side in (-1, 1):
            pass_text(hop, side, "start")
        send_full(0, cuts[hop + 1], cuts[hop + 2])
    for slot in range(1, full):
        send_full(slot, 1, SB)
        keep_head(slot, slot * SB + me)

    def forward_text(phase, peer, places):
        for at in places:

            def forward(step, carry, at=at):
                piece = text_piece(step * PLANE + at)
                pltpu.make_async_remote_copy(
                    src_ref=piece,
                    dst_ref=piece,
                    send_sem=text_send_sem.at[phase],
                    recv_sem=text_recv_sem.at[phase],
                    device_id={"seq": peer},
                    device_id_type=MESH,
                ).start()
                return carry

            lax.fori_loop(0, planes, forward, 0)

    def wait_text(sem, count):
        whole = text.at[:, pl.ds(0, count * text_cols), :]
        pltpu.make_async_copy(whole, whole, sem).wait()

    stripe_len = held.shape[2]
    tile = 2 * rows

    def attend(slot, head):
        band = band_ref[head]
        block_ids = lax.broadcasted_iota(jnp.int32, (1, stripe_len), 1) // rows

        def attend_tile(step, carry):
            at = pl.ds(pl.multiple_of(step * tile, tile), tile)
            scores = lax.dot_general(
                held[slot, 0, at, :], held[slot, 1], NT, preferred_element_type=jnp.float32
            )
            for half in range(2):
                gap = jnp.abs(block_ids - (2 * step + half))
                mask = jnp.where(gap <= band, 0.0, -jnp.inf)
                part = scores[half * rows : (half + 1) * rows] + mask
                top = jnp.max(part, axis=1, keepdims=True)
                weights = jnp.exp2((part - top) * (scale * math.log2(math.e)))
                total = jnp.sum(weights, axis=1, keepdims=True)
                summed = jnp.dot(
                    weights.astype(jnp.bfloat16),
                    held[slot, 2],
                    preferred_element_type=jnp.float32,
                )
                attended[slot, block_rows(2 * step + half), :] = (summed / total).astype(
                    jnp.bfloat16
                )
            return carry

        lax.fori_loop(0, stripe_len // tile, attend_tile, 0)

    def give_back(slot, head):
        def give(step, carry):
            peer = (me + step) % SB
            pltpu.make_async_remote_copy(
                src_ref=attended.at[slot, block_rows(peer), :],
                dst_ref=self_out_ref.at[:, head_cols(head)],
                send_sem=back_send_sem.at[slot],
                recv_sem=back_recv_sem,
                device_id={"seq": stripe + peer},
                device_id_type=MESH,
            ).start()
            return carry

        lax.fori_loop(1, SB, give, 0)
        pltpu.make_async_copy(
            attended.at[slot, block_rows(me), :],
            self_out_ref.at[:, head_cols(head)],
            back_recv_sem,
        ).start()

    def wait_held(slot):
        pltpu.make_async_copy(held.at[slot], held.at[slot], recv_sem.at[slot]).wait()

    def cross():
        def cross_head(head, carry):
            at = pl.ds(pl.multiple_of(head * dim, dim), dim)
            scores = jnp.dot(
                cross_ref[:, at], text[0, at, :], preferred_element_type=jnp.float32
            )
            top = jnp.max(scores, axis=1, keepdims=True)
            weights = jnp.exp2((scores - top) * (scale * math.log2(math.e)))
            total = jnp.sum(weights, axis=1, keepdims=True)
            summed = lax.dot_general(
                weights.astype(jnp.bfloat16), text[1, at, :], NT, preferred_element_type=jnp.float32
            )
            cross_out_ref[:, at] = (summed / total).astype(jnp.bfloat16)
            return carry

        lax.fori_loop(0, heads, cross_head, 0, unroll=4 if heads % 4 == 0 else 1)

    for side in (-1, 1):
        take_text(planes - 2, side)
    forward_text(0, across, (place,))
    if rest:

        @pl.when(mine)
        def _():
            wait_held(full)
            attend(full, full * SB + first)
            give_back(full, full * SB + first)

    wait_text(text_recv_sem.at[0], planes)
    forward_text(1, beside, (place, (1 - place // 2) * 2 + place % 2))
    wait_held(0)
    attend(0, me)
    give_back(0, me)
    wait_text(text_recv_sem.at[1], 2 * planes)
    cross()
    for slot in range(1, full):
        wait_held(slot)
        attend(slot, slot * SB + me)
        give_back(slot, slot * SB + me)
    if rest:

        @pl.when(mine)
        def _():
            done = attended.at[full, pl.ds(0, (SB - 1) * rows), :]
            pltpu.make_async_copy(done, done, back_send_sem.at[full]).wait()

        @pl.when(jnp.logical_not(mine))
        def _():
            sent = held.at[full, :, pl.ds(0, rows), :]
            pltpu.make_async_copy(sent, sent, edge_sem).wait()

        sent = held.at[full, :, pl.ds(0, (rest - 1) * rows), :]
        pltpu.make_async_copy(sent, sent, send_sem.at[full]).wait()

    for slot in range(full):
        sent = held.at[slot, :, pl.ds(0, (SB - 1) * rows), :]
        pltpu.make_async_copy(sent, sent, send_sem.at[slot]).wait()
        done = attended.at[slot, pl.ds(0, (SB - 1) * rows), :]
        pltpu.make_async_copy(done, done, back_send_sem.at[slot]).wait()
    for hop in range(planes - 1):
        for side in (-1, 1):
            pass_text(hop, side, "wait")
    wait_text(text_send_sem.at[0], planes)
    wait_text(text_send_sem.at[1], 2 * planes)
    pltpu.make_async_copy(self_out_ref, self_out_ref, back_recv_sem).wait()


def shards(
    self_query, self_key, self_value, cross_query, context, key_weight, value_weight, band_width
):
    devices = lax.axis_size("seq")
    rows, width = self_query.shape
    heads = band_width.shape[0]
    dim = width // heads
    slots = (heads + SB - 1) // SB
    text_len, depth = context.shape
    text_cols = key_weight.shape[1]
    vmem = pl.BlockSpec(memory_space=pltpu.VMEM)
    hbm = pl.BlockSpec(memory_space=pl.ANY)
    dtype = jnp.bfloat16
    return pl.pallas_call(
        functools.partial(kernel, devices, 1.0 / math.sqrt(dim)),
        out_shape=(
            jax.ShapeDtypeStruct((rows, width), dtype),
            jax.ShapeDtypeStruct((rows, width), dtype),
        ),
        in_specs=[
            pl.BlockSpec(memory_space=pltpu.SMEM),
            hbm,
            hbm,
            hbm,
            vmem,
            hbm,
            hbm,
            hbm,
        ],
        out_specs=(vmem, vmem),
        scratch_shapes=[
            pltpu.VMEM((slots, 3, SB * rows, dim), dtype),
            pltpu.VMEM((slots, SB * rows, dim), dtype),
            pltpu.VMEM((2, width, text_len), dtype),
            pltpu.VMEM((text_len, depth), dtype),
            pltpu.VMEM((2, text_cols, depth), dtype),
            pltpu.SemaphoreType.DMA((3,)),
            pltpu.SemaphoreType.DMA((slots,)),
            pltpu.SemaphoreType.DMA,
            pltpu.SemaphoreType.DMA((slots,)),
            pltpu.SemaphoreType.DMA((slots,)),
            pltpu.SemaphoreType.DMA,
            pltpu.SemaphoreType.DMA((2,)),
            pltpu.SemaphoreType.DMA((2,)),
            pltpu.SemaphoreType.DMA((2, devices // PLANE)),
            pltpu.SemaphoreType.DMA((2, devices // PLANE)),
        ],
        compiler_params=pltpu.CompilerParams(
            collective_id=0, has_side_effects=True, vmem_limit_bytes=56 * 1024 * 1024
        ),
        cost_estimate=pl.CostEstimate(
            flops=4 * slots * (SB * rows) ** 2 * dim,
            bytes_accessed=16 * rows * width,
            transcendentals=slots * (SB * rows) ** 2,
        ),
    )(
        band_width,
        self_query,
        self_key,
        self_value,
        cross_query,
        context,
        key_weight.T,
        value_weight.T,
    )


def solution(mesh):
    in_specs = (
        P(("groups", "seq"), None),
        P(("groups", "seq"), None),
        P(("groups", "seq"), None),
        P(("groups", "seq"), None),
        P("groups", None),
        P(None, "seq"),
        P(None, "seq"),
        P(),
    )
    out_specs = (P(("groups", "seq"), None), P(("groups", "seq"), None))
    return jax.shard_map(shards, mesh=mesh, in_specs=in_specs, out_specs=out_specs, check_vma=False)
```
